512 devices in a mesh: row: 16 (over z, core), col: 32 (over y, x).
Axes of the slice: x: 4, y: 8, z: 8, core: 2. Of those that a mesh axis runs over, the one named last changes fastest.
Arguments:
- features: bfloat16 [65536, 256], P('col', 'row'), may hold values from -6 to 6
- weight: bfloat16 [256, 256], replicated, may hold values from -0.375 to 0.375
- cotangent: bfloat16 [65536, 256], P(('row', 'col')), may hold values from -6 to 6
- tile_values: bfloat16 [16, 32, 96, 128, 128], P('row', 'col'), may hold values from -0.0546875 to 0.0546875
- tile_coords: int32 [16, 32, 96, 2], P('row', 'col'), may hold values from 0 to 31, as said below
- tile_count: int32 [16, 32], P('row', 'col'), may hold values from 24 to 96
Outputs:
- activations: bfloat16 [65536, 256], P(('row', 'col'))
- grad_features: bfloat16 [65536, 256], P('col', 'row')
- grad_weight: float32 [256, 256], replicated
The draws below stay inside these ranges and needn't reach their ends.
Inputs may be any that keep to these rules, and one draw needn't show every extreme that they name: `tile_coords`: within a block the slots name distinct tiles; tile rows are below 32 and tile columns below 16.
All inputs are finite; a program needn't handle non-finite values.
Results may differ from the reference program's by a relative error of at most 0.03.
Values may be sent and summed in bfloat16 or wider, within the bound.
No kernel may reach another device: no remote copies, remote signals or barrier semaphores. Data moves between devices by JAX's collectives and lax.ppermute only.
A program may use at most 64 MiB of HBM per device.

```python
import jax
import jax.numpy as jnp
from jax import lax

F = 256
TILE = 128
NODES = 65536
RT = 32
CT = 16
TILES = 96
N_ROW = 16
N_COL = 32


def draw_tile_coords(key, part):
    key = jax.random.fold_in(key, 11)
    blocks = N_ROW * N_COL
    slot_total = RT * CT
    scores = jax.random.randint(key, (blocks, slot_total), 0, 1 << 20) * slot_total
    scores = scores + jnp.arange(slot_total, dtype=jnp.int32)[None, :]
    _, chosen = lax.top_k(scores, TILES)
    chosen = chosen.astype(jnp.int32)
    coords = jnp.stack([chosen // CT, chosen % CT], axis=-1)
    return coords.reshape(N_ROW, N_COL, TILES, 2).astype(jnp.int32)


def draw_tile_count(key, part):
    key = jax.random.fold_in(key, 23)
    blocks = N_ROW * N_COL
    key_base, key_hot, key_pick = jax.random.split(key, 3)
    base = TILES // 4 + jax.random.randint(key_base, (blocks,), 0, TILES // 4 + 1)
    picked = jax.random.randint(key_pick, (), 0, blocks)
    hot = (jax.random.randint(key_hot, (blocks,), 0, 8) == 0) | (jnp.arange(blocks, dtype=jnp.int32) == picked)
    counts = jnp.where(hot, TILES, base)
    return counts.reshape(N_ROW, N_COL).astype(jnp.int32)


def block_levels(key, shape, cuts, smallest, top_value):
    def one(axis_at, shards_of):
        heights = jax.random.uniform(jax.random.fold_in(jax.random.fold_in(key, 6), axis_at), (shards_of,), jnp.float32, smallest / len(cuts), top_value / len(cuts))
        return jnp.repeat(jnp.exp(heights), shape[axis_at] // shards_of).reshape((-1,) + (1,) * (len(shape) - axis_at - 1))

    level = one(*cuts[0])
    for cut in cuts[1:]:
        level = level * one(*cut)
    return level


def noise(key, dims, scale, limit, pieces=(), kind=jnp.bfloat16):
    array = scale * jax.random.normal(key, dims, jnp.float32)
    if pieces:
        array = array * block_levels(key, dims, pieces, -0.22, 0.18)
    return jnp.clip(array, -limit, limit).astype(kind)


def setup_inputs(seed: int = 0) -> dict:
    arg_keys = jax.random.split(jax.random.key(seed), 7)
    return {
        "features": noise(arg_keys[0], (NODES, F), 1.0, 6.0, ((0, 32), (1, 16))),
        "weight": noise(arg_keys[1], (F, F), F ** -0.5, 0.375),
        "cotangent": noise(arg_keys[2], (NODES, F), 1.0, 6.0, ((0, 512),)),
        "tile_values": noise(arg_keys[3], (N_ROW, N_COL, TILES, TILE, TILE), (TILE * TILES * N_COL // RT) ** -0.5, 0.0546875, ((0, 16), (1, 32))),
        "tile_coords": draw_tile_coords(jax.random.fold_in(arg_keys[6], 71), 0),
        "tile_count": draw_tile_count(jax.random.fold_in(arg_keys[6], 71), 0),
    }


def reference(features, weight, cotangent, tile_values, tile_coords, tile_count):
    blocks = N_ROW * N_COL
    values = tile_values.reshape(blocks, TILES, TILE, TILE)
    coords = tile_coords.reshape(blocks, TILES, 2).astype(jnp.int32)
    counts = tile_count.reshape(blocks).astype(jnp.int32)
    index = jnp.arange(blocks, dtype=jnp.int32)
    row_base = index // N_COL * RT
    col_base = index % N_COL * CT
    slot_ids = jnp.arange(TILES, dtype=jnp.int32)
    row_ids = jnp.arange(RT, dtype=jnp.int32)
    col_ids = jnp.arange(CT, dtype=jnp.int32)
    feat_tiles = features.reshape(NODES // TILE, TILE, F)

    def forward_block(total, item):
        vals, cds, cnt, rbase, cbase = item
        live = (slot_ids < cnt).astype(jnp.float32)
        picked = feat_tiles[cbase + cds[:, 1]].astype(jnp.float32)
        prod = jnp.einsum('tab,tbf->taf', vals.astype(jnp.float32), picked) * live[:, None, None]
        block = jnp.zeros((RT, TILE, F), jnp.float32).at[cds[:, 0]].add(prod)
        block = block.astype(jnp.bfloat16).astype(jnp.float32)
        return (total.at[rbase + row_ids].add(block), None)
    summed, _ = lax.scan(forward_block, jnp.zeros((NODES // TILE, TILE, F), jnp.float32), (values, coords, counts, row_base, col_base))
    summed = summed.reshape(NODES, F).astype(jnp.bfloat16)
    pre = jnp.dot(summed, weight, preferred_element_type=jnp.float32)

    def activate(v):
        return jax.nn.gelu(v, approximate=True)
    out, back = jax.vjp(activate, pre)
    activations = out.astype(jnp.bfloat16)
    grad_pre = back(cotangent.astype(jnp.float32))[0].astype(jnp.bfloat16)
    grad_weight = jnp.dot(summed.T, grad_pre, preferred_element_type=jnp.float32)
    grad_summed = jnp.dot(grad_pre, weight.T, preferred_element_type=jnp.float32).astype(jnp.bfloat16)
    grad_tiles = grad_summed.reshape(NODES // TILE, TILE, F)

    def backward_block(total, item):
        vals, cds, cnt, rbase, cbase = item
        live = (slot_ids < cnt).astype(jnp.float32)
        picked = grad_tiles[rbase + cds[:, 0]].astype(jnp.float32)
        prod = jnp.einsum('tab,taf->tbf', vals.astype(jnp.float32), picked) * live[:, None, None]
        block = jnp.zeros((CT, TILE, F), jnp.float32).at[cds[:, 1]].add(prod)
        block = block.astype(jnp.bfloat16).astype(jnp.float32)
        return (total.at[cbase + col_ids].add(block), None)
    grad_x, _ = lax.scan(backward_block, jnp.zeros((NODES // TILE, TILE, F), jnp.float32), (values, coords, counts, row_base, col_base))
    grad_features = grad_x.reshape(NODES, F).astype(jnp.bfloat16)
    return (activations, grad_features, grad_weight)
```

```python
import jax
import jax.numpy as jnp
from jax import lax
from jax.experimental import pallas as pl
from jax.experimental.pallas import tpu as pltpu
from jax.sharding import Mesh, PartitionSpec as P

BF = jnp.bfloat16
F32 = jnp.float32
SMEM = pl.BlockSpec(memory_space=pltpu.SMEM)
VMEM = pl.BlockSpec(memory_space=pltpu.VMEM)
AXES = ("z", "core", "y", "x")
NZ, NC, NY, NX = 8, 2, 8, 4
NL = 2
NH = NY // NL
NEAR = NL * NX
SHARE = 16
TERMS = 64
UNROLL = 8


def device(z, core, y, x):
    return ((z * NC + core) * NY + y) * NX + x


def turned(i, core, n):
    return i if core == 0 else (n - i) % n


def near_groups():
    return [
        [device(z, core, h * NL + d // NX, d % NX) for d in range(NEAR)]
        for z in range(NZ)
        for core in range(NC)
        for h in range(NH)
    ]


def far_groups():
    return [
        [device(z, core, turned(h, core, NH) * NL + d // NX, d % NX) for h in range(NH)]
        for z in range(NZ)
        for core in range(NC)
        for d in range(NEAR)
    ]


def depth_groups():
    return [
        [device(turned(z, core, NZ), core, y, x) for z in range(NZ)]
        for core in range(NC)
        for y in range(NY)
        for x in range(NX)
    ]


def exchange(x, groups):
    return lax.all_to_all(x, AXES, 0, 0, axis_index_groups=groups, tiled=True)


def place(i, core, n):
    return jnp.where(core == 0, i, (n - i) % n)


def forward_kernel(coords, info, own, other, vals, out, panel, acc):
    tile = vals.shape[1]
    count, core = info[0], info[1]
    for b in range(panel.shape[0] // tile):
        cols = slice(b * tile, (b + 1) * tile)
        for part, owner in ((own, core), (other, 1 - core)):
            slab = jnp.concatenate([part[place(z, owner, NZ), :, cols] for z in range(NZ)], axis=0)
            at = pl.multiple_of(owner * tile, tile)
            panel[cols, pl.ds(at, tile)] = slab.T
    acc[...] = jnp.zeros_like(acc)

    def step(g, carry):
        prods = []
        for u in range(UNROLL):
            s = g * UNROLL + u
            c = pl.multiple_of(coords[2 * s + 1] * tile, tile)
            prods.append(jnp.dot(vals[s], panel[pl.ds(c, tile), :], preferred_element_type=F32))
        for u in range(UNROLL):
            r = coords[2 * (g * UNROLL + u)]
            acc[r] += prods[u]
        return carry

    lax.fori_loop(0, (count + UNROLL - 1) // UNROLL, step, 0)
    for h in range(NH):
        at = place(h, core, NH)
        for d in range(NEAR):
            out[d, at] = acc[h * NEAR + d].astype(BF)


def add_kernel(parts, out):
    out[...] = jnp.sum(parts[...].astype(F32), axis=0).astype(BF)


def dense_kernel(info, parts, weight, cot, act, sent, scratch):
    core = info[1]
    width = weight.shape[0]
    order = [(2 * z + c) * SHARE for c in range(NC) for z in range(NZ)]
    s = jnp.sum(parts[...].astype(F32), axis=0).astype(BF)
    w = jnp.concatenate([weight[a : a + SHARE, :] for a in order], axis=0)
    v = jnp.dot(s, w, preferred_element_type=F32)
    k = 0.7978845608028654
    t = jnp.tanh(k * (v + 0.044715 * (v * v * v)))
    act[...] = (0.5 * v * (1.0 + t)).astype(BF)
    slope = 0.5 * (1.0 + t) + 0.5 * v * (1.0 - t * t) * (k * (1.0 + 3.0 * 0.044715 * v * v))
    g = (cot[...].astype(F32) * slope).astype(BF)
    back = lax.dot_general(w, g, (((1,), (1,)), ((), ())), preferred_element_type=F32).astype(BF)
    terms = lax.dot_general(s, g, (((0,), (0,)), ((), ())), preferred_element_type=F32)
    for i, a in enumerate(order):
        scratch[a : a + SHARE, :] = terms[i * SHARE : (i + 1) * SHARE, :]
    half = back.shape[1]
    rows = width // NH
    for h in range(NH):
        at = place(h, core, NH)
        sent[at, :width, :] = back
        sent[at, width : width + rows, :] = scratch[rows * h : rows * (h + 1), :half].astype(BF)
        sent[at, width + rows :, :] = scratch[rows * h : rows * (h + 1), half:].astype(BF)


def spread_kernel(got, sent):
    width = got.shape[1] - 2 * TERMS
    terms = jnp.sum(got[:, width:, :].astype(F32), axis=0)
    for d in range(NEAR):
        for h in range(NH):
            sent[d, h * width : (h + 1) * width, :] = got[h, :width, :]
        piece = jnp.concatenate([terms[8 * d : 8 * d + 8], terms[TERMS + 8 * d : TERMS + 8 * d + 8]], axis=0)
        sent[d, NH * width :, :] = piece.astype(BF)


def backward_kernel(coords, info, panel, vals, mine, theirs, acc):
    count, core = info[0], info[1]
    tiles, width, tile = acc.shape
    acc[...] = jnp.zeros_like(acc)

    def step(g, carry):
        prods = []
        for u in range(UNROLL):
            s = g * UNROLL + u
            r = coords[2 * s]
            h = pl.multiple_of(place(lax.div(r, NEAR), core, NH) * width, width)
            prods.append(jnp.dot(panel[lax.rem(r, NEAR), pl.ds(h, width), :], vals[s], preferred_element_type=F32))
        for u in range(UNROLL):
            c = coords[2 * (g * UNROLL + u) + 1]
            acc[c] += prods[u]
        return carry

    lax.fori_loop(0, (count + UNROLL - 1) // UNROLL, step, 0)
    terms = jnp.sum(panel[:, NH * width :, :].astype(F32), axis=0).astype(BF)
    for out, owner in ((mine, core), (theirs, 1 - core)):
        for z in range(NZ):
            a = pl.multiple_of(owner * tile + z * SHARE, SHARE)
            at = place(z, owner, NZ)
            for c in range(tiles):
                out[at, SHARE * c : SHARE * (c + 1), :] = acc[c, pl.ds(a, SHARE), :].astype(BF)
            out[at, SHARE * tiles :, :] = terms


def params(mib):
    return pltpu.CompilerParams(vmem_limit_bytes=mib * 1024 * 1024)


def body(features, weight, cotangent, tile_values, tile_coords, tile_count):
    coords = tile_coords.reshape(-1)
    core = lax.axis_index("core").astype(jnp.int32)
    nodes, share = features.shape
    slots, tile = tile_values.shape[2:4]
    width = weight.shape[0]
    row_tiles = NY * NX
    col_tiles = nodes // tile
    swap = ((0, 1), (1, 0))

    own = jnp.broadcast_to(features.T[None], (NZ, share, nodes))
    own = exchange(own, depth_groups())
    own, count = lax.optimization_barrier((own, tile_count[0, 0]))
    other = lax.ppermute(own, "core", swap)
    live = lax.broadcasted_iota(jnp.int32, (slots, tile, tile), 0) < count
    vals = jnp.where(live, tile_values[0, 0], jnp.zeros((), BF))
    info = jnp.stack([count, core])
    sums = pl.pallas_call(
        forward_kernel,
        out_shape=jax.ShapeDtypeStruct((NEAR, NH, tile, width), BF),
        in_specs=[SMEM, SMEM, VMEM, VMEM, VMEM],
        out_specs=VMEM,
        scratch_shapes=[pltpu.VMEM((nodes, width), BF), pltpu.VMEM((row_tiles, tile, width), F32)],
        compiler_params=params(24),
        name="forward_tiles",
    )(coords, info, own, other, vals)
    parts = exchange(sums, near_groups())
    parts = pl.pallas_call(
        add_kernel,
        out_shape=jax.ShapeDtypeStruct((NH, tile, width), BF),
        in_specs=[VMEM],
        out_specs=VMEM,
        compiler_params=params(24),
        name="add_near",
    )(parts)
    parts = exchange(parts, far_groups())
    activations, sent = pl.pallas_call(
        dense_kernel,
        out_shape=(
            jax.ShapeDtypeStruct((tile, width), BF),
            jax.ShapeDtypeStruct((NH, width + 2 * TERMS, tile), BF),
        ),
        in_specs=[SMEM, VMEM, VMEM, VMEM],
        out_specs=(VMEM, VMEM),
        scratch_shapes=[pltpu.VMEM((width, width), F32)],
        compiler_params=params(24),
        name="dense",
    )(info, parts, weight, cotangent)
    got = exchange(sent, far_groups())
    sent = pl.pallas_call(
        spread_kernel,
        out_shape=jax.ShapeDtypeStruct((NEAR, NH * width + 16, tile), BF),
        in_specs=[VMEM],
        out_specs=VMEM,
        compiler_params=params(24),
        name="spread_near",
    )(got)
    panel = exchange(sent, near_groups())
    mine, theirs = pl.pallas_call(
        backward_kernel,
        out_shape=(jax.ShapeDtypeStruct((NZ, width + 16, tile), BF),) * 2,
        in_specs=[SMEM, SMEM, VMEM, VMEM],
        out_specs=(VMEM, VMEM),
        scratch_shapes=[pltpu.VMEM((col_tiles, width, tile), F32)],
        compiler_params=params(24),
        name="backward_tiles",
    )(coords, info, panel, vals)
    got = lax.ppermute(theirs, "core", swap)
    both = (mine.astype(F32) + got.astype(F32)).astype(BF)
    back = exchange(both, depth_groups())
    back = jnp.sum(back.astype(F32), axis=0)
    piece = back[width:]
    grad_features = back[:width].astype(BF).reshape(col_tiles, share, tile)
    grad_features = grad_features.transpose(0, 2, 1).reshape(nodes, share)
    whole = jnp.broadcast_to(piece[None], (row_tiles,) + piece.shape)
    whole = lax.all_to_all(whole, ("y", "x"), 0, 0, tiled=True)
    grad_weight = whole.reshape(row_tiles, 2, 8, tile).transpose(0, 2, 1, 3).reshape(width, width)
    return (activations, grad_features, grad_weight)


def solution(mesh):
    fine = Mesh(mesh.devices.reshape(NZ, NC, NY, NX), AXES)
    row, col = AXES[:2], AXES[2:]
    placed = (
        P(col, row),
        P(),
        P(row + col, None),
        P(row, col, None, None, None),
        P(row, col, None, None),
        P(row, col),
    )
    return jax.shard_map(
        body,
        mesh=fine,
        in_specs=placed,
        out_specs=(P(row + col, None), P(col, row), P()),
        check_vma=False,
    )
```

```python
import jax
import jax.numpy as jnp
from jax import lax
from jax.experimental import pallas as pl
from jax.experimental.pallas import tpu as pltpu
from jax.sharding import Mesh, PartitionSpec as P

BF = jnp.bfloat16
F32 = jnp.float32
SMEM = pl.BlockSpec(memory_space=pltpu.SMEM)
VMEM = pl.BlockSpec(memory_space=pltpu.VMEM)
AXES = ("z", "core", "y", "x")
NZ, NC, NY, NX = 8, 2, 8, 4
SHARE = 16
QUAD = 4
BLOCKS = NY * NX // QUAD
TERMS = 2 * 32
UNROLL = 8


def device(z, core, y, x):
    return ((z * NC + core) * NY + y) * NX + x


def turned(i, core, n):
    return i if core == 0 else (n - i) % n


def quad(core, n, f):
    y = (f // 2 * 2 + n // 2 + core) % NY
    x = (f % 2 * 2 + n % 2 + core) % NX
    return y * NX + x


def spot_of(r, core):
    y, x = (r // NX - core) % NY, (r % NX - core) % NX
    return (y % 2 * 2 + x % 2) * BLOCKS + y // 2 * 2 + x // 2


def quad_groups():
    return [
        [device(z, core, *divmod(quad(core, n, f), NX)) for n in range(QUAD)]
        for z in range(NZ)
        for core in range(NC)
        for f in range(BLOCKS)
    ]


def block_groups():
    return [
        [device(z, core, *divmod(quad(core, n, f), NX)) for f in range(BLOCKS)]
        for z in range(NZ)
        for core in range(NC)
        for n in range(QUAD)
    ]


def depth_groups():
    return [
        [device(turned(z, core, NZ), core, y, x) for z in range(NZ)]
        for core in range(NC)
        for y in range(NY)
        for x in range(NX)
    ]


def exchange(x, groups):
    return lax.all_to_all(x, AXES, 0, 0, axis_index_groups=groups, tiled=True)


def place(i, core, n):
    return jnp.where(core == 0, i, (n - i) % n)


def forward_kernel(coords, info, own, other, vals, out, panel, acc):
    tile = vals.shape[1]
    count, core = info[0], info[1]
    for b in range(panel.shape[0] // tile):
        cols = slice(b * tile, (b + 1) * tile)
        for part, owner in ((own, core), (other, 1 - core)):
            slab = jnp.concatenate([part[place(z, owner, NZ), :, cols] for z in range(NZ)], axis=0)
            at = pl.multiple_of(owner * tile, tile)
            panel[cols, pl.ds(at, tile)] = slab.T
    acc[...] = jnp.zeros_like(acc)

    def step(g, carry):
        prods = []
        for u in range(UNROLL):
            s = g * UNROLL + u
            c = pl.multiple_of(coords[2 * s + 1] * tile, tile)
            prods.append(jnp.dot(vals[s], panel[pl.ds(c, tile), :], preferred_element_type=F32))
        for u in range(UNROLL):
            r = coords[2 * (g * UNROLL + u)]
            acc[r] += prods[u]
        return carry

    lax.fori_loop(0, (count + UNROLL - 1) // UNROLL, step, 0)
    for n in range(QUAD):
        for f in range(BLOCKS):
            out[n, f] = acc[n * BLOCKS + f].astype(BF)


def add_kernel(parts, out):
    out[...] = jnp.sum(parts[...].astype(F32), axis=0).astype(BF)


def dense_kernel(info, parts, weight, cot, act, grads, sent, scratch):
    core = info[1]
    width = weight.shape[0]
    order = [(2 * z + c) * SHARE for c in range(NC) for z in range(NZ)]
    s = jnp.sum(parts[...].astype(F32), axis=0).astype(BF)
    w = jnp.concatenate([weight[a : a + SHARE, :] for a in order], axis=0)
    v = jnp.dot(s, w, preferred_element_type=F32)
    k = 0.7978845608028654
    t = jnp.tanh(k * (v + 0.044715 * (v * v * v)))
    act[...] = (0.5 * v * (1.0 + t)).astype(BF)
    slope = 0.5 * (1.0 + t) + 0.5 * v * (1.0 - t * t) * (k * (1.0 + 3.0 * 0.044715 * v * v))
    g = (cot[...].astype(F32) * slope).astype(BF)
    back = lax.dot_general(w, g, (((1,), (1,)), ((), ())), preferred_element_type=F32).astype(BF)
    terms = lax.dot_general(s, g, (((0,), (0,)), ((), ())), preferred_element_type=F32)
    for i, a in enumerate(order):
        scratch[a : a + SHARE, :] = terms[i * SHARE : (i + 1) * SHARE, :]
    half = back.shape[1]
    rows = width // NZ
    grads[...] = back
    for z in range(NZ):
        at = place(z, core, NZ)
        sent[at, :rows, :] = scratch[rows * z : rows * (z + 1), :half].astype(BF)
        sent[at, rows:, :] = scratch[rows * z : rows * (z + 1), half:].astype(BF)


def pack_kernel(grads, terms, sent):
    width = grads.shape[0]
    piece = jnp.sum(terms[...].astype(F32), axis=0).astype(BF)
    for f in range(BLOCKS):
        sent[f, :width, :] = grads[...]
        sent[f, width:, :] = piece


def spread_kernel(got, sent):
    width = got.shape[1] - TERMS
    piece = jnp.sum(got[:, width:, :].astype(F32), axis=0).astype(BF)
    for n in range(QUAD):
        for f in range(BLOCKS):
            sent[n, f * width : (f + 1) * width, :] = got[f, :width, :]
        sent[n, BLOCKS * width :, :] = piece


def backward_kernel(coords, info, panel, vals, mine, theirs, acc):
    count, core = info[0], info[1]
    tiles, width, tile = acc.shape
    acc[...] = jnp.zeros_like(acc)

    def step(g, carry):
        prods = []
        for u in range(UNROLL):
            s = g * UNROLL + u
            spot = coords[2 * s]
            at = pl.multiple_of(lax.rem(spot, BLOCKS) * width, width)
            prods.append(jnp.dot(panel[lax.div(spot, BLOCKS), pl.ds(at, width), :], vals[s], preferred_element_type=F32))
        for u in range(UNROLL):
            c = coords[2 * (g * UNROLL + u) + 1]
            acc[c] += prods[u]
        return carry

    lax.fori_loop(0, (count + UNROLL - 1) // UNROLL, step, 0)
    terms = jnp.sum(panel[:, BLOCKS * width :, :].astype(F32), axis=0).astype(BF)
    for out, owner in ((mine, core), (theirs, 1 - core)):
        for z in range(NZ):
            a = pl.multiple_of(owner * tile + z * SHARE, SHARE)
            at = place(z, owner, NZ)
            for c in range(tiles):
                out[at, SHARE * c : SHARE * (c + 1), :] = acc[c, pl.ds(a, SHARE), :].astype(BF)
            out[at, SHARE * tiles :, :] = terms


def finish_kernel(info, got, grads, weights):
    core = info[1]
    share, tile = SHARE, got.shape[2]
    width = got.shape[1] - TERMS
    rows = TERMS // 2
    total = jnp.sum(got[:, :width, :].astype(F32), axis=0).astype(BF)
    for c in range(width // share):
        grads[:, c * tile : (c + 1) * tile] = total[c * share : (c + 1) * share, :]
    for z in range(NZ):
        at = place(z, core, NZ)
        weights[rows * z : rows * (z + 1), :tile] = got[at, width : width + rows, :].astype(F32)
        weights[rows * z : rows * (z + 1), tile:] = got[at, width + rows :, :].astype(F32)


def params(mib):
    return pltpu.CompilerParams(vmem_limit_bytes=mib * 1024 * 1024)


def body(features, weight, cotangent, tile_values, tile_coords, tile_count):
    core = lax.axis_index("core").astype(jnp.int32)
    nodes, share = features.shape
    slots, tile = tile_values.shape[2:4]
    width = weight.shape[0]
    row_tiles = NY * NX
    col_tiles = nodes // tile
    swap = ((0, 1), (1, 0))

    own = jnp.broadcast_to(features.T[None], (NZ, share, nodes))
    own = exchange(own, depth_groups())
    own, count, coords = lax.optimization_barrier((own, tile_count[0, 0], tile_coords))
    coords = jnp.stack([spot_of(coords[0, 0, :, 0], core), coords[0, 0, :, 1]], axis=-1).reshape(-1)
    other = lax.ppermute(own, "core", swap)
    live = lax.broadcasted_iota(jnp.int32, (slots, tile, tile), 0) < count
    vals = jnp.where(live, tile_values[0, 0], jnp.zeros((), BF))
    info = jnp.stack([count, core])
    sums = pl.pallas_call(
        forward_kernel,
        out_shape=jax.ShapeDtypeStruct((QUAD, BLOCKS, tile, width), BF),
        in_specs=[SMEM, SMEM, VMEM, VMEM, VMEM],
        out_specs=VMEM,
        scratch_shapes=[pltpu.VMEM((nodes, width), BF), pltpu.VMEM((row_tiles, tile, width), F32)],
        compiler_params=params(24),
        name="forward_tiles",
    )(coords, info, own, other, vals)
    parts = exchange(sums, quad_groups())
    parts = pl.pallas_call(
        add_kernel,
        out_shape=jax.ShapeDtypeStruct((BLOCKS, tile, width), BF),
        in_specs=[VMEM],
        out_specs=VMEM,
        compiler_params=params(24),
        name="add_quad",
    )(parts)
    parts = exchange(parts, block_groups())
    activations, grads, terms = pl.pallas_call(
        dense_kernel,
        out_shape=(
            jax.ShapeDtypeStruct((tile, width), BF),
            jax.ShapeDtypeStruct((width, tile), BF),
            jax.ShapeDtypeStruct((NZ, TERMS, tile), BF),
        ),
        in_specs=[SMEM, VMEM, VMEM, VMEM],
        out_specs=(VMEM, VMEM, VMEM),
        scratch_shapes=[pltpu.VMEM((width, width), F32)],
        compiler_params=params(24),
        name="dense",
    )(info, parts, weight, cotangent)
    terms = exchange(terms, depth_groups())
    sent = pl.pallas_call(
        pack_kernel,
        out_shape=jax.ShapeDtypeStruct((BLOCKS, width + TERMS, tile), BF),
        in_specs=[VMEM, VMEM],
        out_specs=VMEM,
        compiler_params=params(24),
        name="pack",
    )(grads, terms)
    got = exchange(sent, block_groups())
    sent = pl.pallas_call(
        spread_kernel,
        out_shape=jax.ShapeDtypeStruct((QUAD, BLOCKS * width + TERMS, tile), BF),
        in_specs=[VMEM],
        out_specs=VMEM,
        compiler_params=params(24),
        name="spread_quad",
    )(got)
    panel = exchange(sent, quad_groups())
    mine, theirs = pl.pallas_call(
        backward_kernel,
        out_shape=(jax.ShapeDtypeStruct((NZ, width + TERMS, tile), BF),) * 2,
        in_specs=[SMEM, SMEM, VMEM, VMEM],
        out_specs=(VMEM, VMEM),
        scratch_shapes=[pltpu.VMEM((col_tiles, width, tile), F32)],
        compiler_params=params(24),
        name="backward_tiles",
    )(coords, info, panel, vals)
    got = lax.ppermute(theirs, "core", swap)
    both = (mine.astype(F32) + got.astype(F32)).astype(BF)
    back = exchange(both, depth_groups())
    grad_features, grad_weight = pl.pallas_call(
        finish_kernel,
        out_shape=(jax.ShapeDtypeStruct((share, nodes), BF), jax.ShapeDtypeStruct((width, width), F32)),
        in_specs=[SMEM, VMEM],
        out_specs=(VMEM, VMEM),
        compiler_params=params(24),
        name="finish",
    )(info, back)
    grad_features = grad_features.T
    return (activations, grad_features, grad_weight)


def solution(mesh):
    fine = Mesh(mesh.devices.reshape(NZ, NC, NY, NX), AXES)
    row, col = AXES[:2], AXES[2:]
    placed = (
        P(col, row),
        P(),
        P(row + col, None),
        P(row, col, None, None, None),
        P(row, col, None, None),
        P(row, col),
    )
    return jax.shard_map(
        body,
        mesh=fine,
        in_specs=placed,
        out_specs=(P(row + col, None), P(col, row), P()),
        check_vma=False,
    )
```

```python
import jax
import jax.numpy as jnp
from jax import lax
from jax.experimental import pallas as pl
from jax.experimental.pallas import tpu as pltpu
from jax.sharding import Mesh, PartitionSpec as P

BF = jnp.bfloat16
F32 = jnp.float32
SMEM = pl.BlockSpec(memory_space=pltpu.SMEM)
VMEM = pl.BlockSpec(memory_space=pltpu.VMEM)
AXES = ("z", "core", "y", "x")
NZ, NC, NY, NX = 8, 2, 8, 4
SHARE = 16
QUAD = 4
BLOCKS = NY * NX // QUAD
TERMS = 2 * 32
UNROLL = 32


def device(z, core, y, x):
    return ((z * NC + core) * NY + y) * NX + x


def turned(i, core, n):
    return i if core == 0 else (n - i) % n


def quad(core, n, f):
    y = (f // 2 * 2 + n // 2 + core) % NY
    x = (f % 2 * 2 + n % 2 + core) % NX
    return y * NX + x


def spot_of(r, core):
    y, x = (r // NX - core) % NY, (r % NX - core) % NX
    return (y % 2 * 2 + x % 2) * BLOCKS + y // 2 * 2 + x // 2


def quad_groups():
    return [
        [device(z, core, *divmod(quad(core, n, f), NX)) for n in range(QUAD)]
        for z in range(NZ)
        for core in range(NC)
        for f in range(BLOCKS)
    ]


def block_groups():
    return [
        [device(z, core, *divmod(quad(core, n, f), NX)) for f in range(BLOCKS)]
        for z in range(NZ)
        for core in range(NC)
        for n in range(QUAD)
    ]


def depth_groups():
    return [
        [device(turned(z, core, NZ), core, y, x) for z in range(NZ)]
        for core in range(NC)
        for y in range(NY)
        for x in range(NX)
    ]


def exchange(x, groups):
    return lax.all_to_all(x, AXES, 0, 0, axis_index_groups=groups, tiled=True)


def place(i, core, n):
    return jnp.where(core == 0, i, (n - i) % n)


def forward_kernel(coords, info, own, other, vals, out, panel, acc):
    tile = vals.shape[1]
    count, core = info[0], info[1]
    for b in range(panel.shape[0] // tile):
        cols = slice(b * tile, (b + 1) * tile)
        for part, owner in ((own, core), (other, 1 - core)):
            slab = jnp.concatenate([part[place(z, owner, NZ), :, cols] for z in range(NZ)], axis=0)
            at = pl.multiple_of(owner * tile, tile)
            panel[cols, pl.ds(at, tile)] = slab.T
    acc[...] = jnp.zeros_like(acc)

    def step(g, carry):
        prods = []
        for u in range(UNROLL):
            s = g * UNROLL + u
            c = pl.multiple_of(coords[2 * s + 1] * tile, tile)
            prods.append(jnp.dot(vals[s], panel[pl.ds(c, tile), :], preferred_element_type=F32))
        for u in range(UNROLL):
            r = coords[2 * (g * UNROLL + u)]
            acc[r] += prods[u]
        return carry

    lax.fori_loop(0, (count + UNROLL - 1) // UNROLL, step, 0)
    for n in range(QUAD):
        for f in range(BLOCKS):
            out[n, f] = acc[n * BLOCKS + f].astype(BF)


def add_kernel(parts, out):
    out[...] = jnp.sum(parts[...].astype(F32), axis=0).astype(BF)


def dense_kernel(info, parts, weight, cot, act, grads, sent, scratch):
    core = info[1]
    width = weight.shape[0]
    order = [(2 * z + c) * SHARE for c in range(NC) for z in range(NZ)]
    s = jnp.sum(parts[...].astype(F32), axis=0).astype(BF)
    w = jnp.concatenate([weight[a : a + SHARE, :] for a in order], axis=0)
    v = jnp.dot(s, w, preferred_element_type=F32)
    k = 0.7978845608028654
    t = jnp.tanh(k * (v + 0.044715 * (v * v * v)))
    act[...] = (0.5 * v * (1.0 + t)).astype(BF)
    slope = 0.5 * (1.0 + t) + 0.5 * v * (1.0 - t * t) * (k * (1.0 + 3.0 * 0.044715 * v * v))
    g = (cot[...].astype(F32) * slope).astype(BF)
    back = lax.dot_general(w, g, (((1,), (1,)), ((), ())), preferred_element_type=F32).astype(BF)
    terms = lax.dot_general(s, g, (((0,), (0,)), ((), ())), preferred_element_type=F32)
    for i, a in enumerate(order):
        scratch[a : a + SHARE, :] = terms[i * SHARE : (i + 1) * SHARE, :]
    half = back.shape[1]
    rows = width // NZ
    grads[...] = back
    for z in range(NZ):
        at = place(z, core, NZ)
        sent[at, :rows, :] = scratch[rows * z : rows * (z + 1), :half].astype(BF)
        sent[at, rows:, :] = scratch[rows * z : rows * (z + 1), half:].astype(BF)


def pack_kernel(grads, terms, sent):
    width = grads.shape[0]
    piece = jnp.sum(terms[...].astype(F32), axis=0).astype(BF)
    for f in range(BLOCKS):
        sent[f, :width, :] = grads[...]
        sent[f, width:, :] = piece


def spread_kernel(got, sent):
    width = got.shape[1] - TERMS
    piece = jnp.sum(got[:, width:, :].astype(F32), axis=0).astype(BF)
    for n in range(QUAD):
        for f in range(BLOCKS):
            sent[n, f * width : (f + 1) * width, :] = got[f, :width, :]
        sent[n, BLOCKS * width :, :] = piece


def backward_kernel(coords, info, panel, vals, mine, theirs, acc):
    count, core = info[0], info[1]
    tiles, width, tile = acc.shape
    acc[...] = jnp.zeros_like(acc)

    def step(g, carry):
        prods = []
        for u in range(UNROLL):
            s = g * UNROLL + u
            spot = coords[2 * s]
            at = pl.multiple_of(lax.rem(spot, BLOCKS) * width, width)
            prods.append(jnp.dot(panel[lax.div(spot, BLOCKS), pl.ds(at, width), :], vals[s], preferred_element_type=F32))
        for u in range(UNROLL):
            c = coords[2 * (g * UNROLL + u) + 1]
            acc[c] += prods[u]
        return carry

    lax.fori_loop(0, (count + UNROLL - 1) // UNROLL, step, 0)
    terms = jnp.sum(panel[:, BLOCKS * width :, :].astype(F32), axis=0).astype(BF)
    for out, owner in ((mine, core), (theirs, 1 - core)):
        for z in range(NZ):
            a = pl.multiple_of(owner * tile + z * SHARE, SHARE)
            at = place(z, owner, NZ)
            for c in range(tiles):
                out[at, SHARE * c : SHARE * (c + 1), :] = acc[c, pl.ds(a, SHARE), :].astype(BF)
            out[at, SHARE * tiles :, :] = terms


def finish_kernel(info, got, grads, weights):
    core = info[1]
    share, tile = SHARE, got.shape[2]
    width = got.shape[1] - TERMS
    rows = TERMS // 2
    total = jnp.sum(got[:, :width, :].astype(F32), axis=0).astype(BF)
    for c in range(width // share):
        grads[:, c * tile : (c + 1) * tile] = total[c * share : (c + 1) * share, :]
    for z in range(NZ):
        at = place(z, core, NZ)
        weights[rows * z : rows * (z + 1), :tile] = got[at, width : width + rows, :].astype(F32)
        weights[rows * z : rows * (z + 1), tile:] = got[at, width + rows :, :].astype(F32)


def params(mib):
    return pltpu.CompilerParams(vmem_limit_bytes=mib * 1024 * 1024)


def body(features, weight, cotangent, tile_values, tile_coords, tile_count):
    core = lax.axis_index("core").astype(jnp.int32)
    nodes, share = features.shape
    slots, tile = tile_values.shape[2:4]
    width = weight.shape[0]
    row_tiles = NY * NX
    col_tiles = nodes // tile
    swap = ((0, 1), (1, 0))

    own = jnp.broadcast_to(features.T[None], (NZ, share, nodes))
    own = exchange(own, depth_groups())
    count, coords = tile_count[0, 0], tile_coords
    coords = jnp.stack([spot_of(coords[0, 0, :, 0], core), coords[0, 0, :, 1]], axis=-1).reshape(-1)
    other = lax.ppermute(own, "core", swap)
    live = lax.broadcasted_iota(jnp.int32, (slots, tile, tile), 0) < count
    vals = jnp.where(live, tile_values[0, 0], jnp.zeros((), BF))
    info = jnp.stack([count, core])
    sums = pl.pallas_call(
        forward_kernel,
        out_shape=jax.ShapeDtypeStruct((QUAD, BLOCKS, tile, width), BF),
        in_specs=[SMEM, SMEM, VMEM, VMEM, VMEM],
        out_specs=VMEM,
        scratch_shapes=[pltpu.VMEM((nodes, width), BF), pltpu.VMEM((row_tiles, tile, width), F32)],
        compiler_params=params(24),
        name="forward_tiles",
    )(coords, info, own, other, vals)
    parts = exchange(sums, quad_groups())
    parts = pl.pallas_call(
        add_kernel,
        out_shape=jax.ShapeDtypeStruct((BLOCKS, tile, width), BF),
        in_specs=[VMEM],
        out_specs=VMEM,
        compiler_params=params(24),
        name="add_quad",
    )(parts)
    parts = exchange(parts, block_groups())
    activations, grads, terms = pl.pallas_call(
        dense_kernel,
        out_shape=(
            jax.ShapeDtypeStruct((tile, width), BF),
            jax.ShapeDtypeStruct((width, tile), BF),
            jax.ShapeDtypeStruct((NZ, TERMS, tile), BF),
        ),
        in_specs=[SMEM, VMEM, VMEM, VMEM],
        out_specs=(VMEM, VMEM, VMEM),
        scratch_shapes=[pltpu.VMEM((width, width), F32)],
        compiler_params=params(24),
        name="dense",
    )(info, parts, weight, cotangent)
    terms = exchange(terms, depth_groups())
    sent = pl.pallas_call(
        pack_kernel,
        out_shape=jax.ShapeDtypeStruct((BLOCKS, width + TERMS, tile), BF),
        in_specs=[VMEM, VMEM],
        out_specs=VMEM,
        compiler_params=params(24),
        name="pack",
    )(grads, terms)
    got = exchange(sent, block_groups())
    sent = pl.pallas_call(
        spread_kernel,
        out_shape=jax.ShapeDtypeStruct((QUAD, BLOCKS * width + TERMS, tile), BF),
        in_specs=[VMEM],
        out_specs=VMEM,
        compiler_params=params(24),
        name="spread_quad",
    )(got)
    panel = exchange(sent, quad_groups())
    mine, theirs = pl.pallas_call(
        backward_kernel,
        out_shape=(jax.ShapeDtypeStruct((NZ, width + TERMS, tile), BF),) * 2,
        in_specs=[SMEM, SMEM, VMEM, VMEM],
        out_specs=(VMEM, VMEM),
        scratch_shapes=[pltpu.VMEM((col_tiles, width, tile), F32)],
        compiler_params=params(24),
        name="backward_tiles",
    )(coords, info, panel, vals)
    got = lax.ppermute(theirs, "core", swap)
    both = (mine.astype(F32) + got.astype(F32)).astype(BF)
    back = exchange(both, depth_groups())
    grad_features, grad_weight = pl.pallas_call(
        finish_kernel,
        out_shape=(jax.ShapeDtypeStruct((share, nodes), BF), jax.ShapeDtypeStruct((width, width), F32)),
        in_specs=[SMEM, VMEM],
        out_specs=(VMEM, VMEM),
        compiler_params=params(24),
        name="finish",
    )(info, back)
    grad_features = grad_features.T
    return (activations, grad_features, grad_weight)


def solution(mesh):
    fine = Mesh(mesh.devices.reshape(NZ, NC, NY, NX), AXES)
    row, col = AXES[:2], AXES[2:]
    placed = (
        P(col, row),
        P(),
        P(row + col, None),
        P(row, col, None, None, None),
        P(row, col, None, None),
        P(row, col),
    )
    return jax.shard_map(
        body,
        mesh=fine,
        in_specs=placed,
        out_specs=(P(row + col, None), P(col, row), P()),
        check_vma=False,
    )
```

```python
import jax
import jax.numpy as jnp
from jax import lax
from jax.experimental import pallas as pl
from jax.experimental.pallas import tpu as pltpu
from jax.sharding import Mesh, PartitionSpec as P

BF = jnp.bfloat16
F32 = jnp.float32
SMEM = pl.BlockSpec(memory_space=pltpu.SMEM)
VMEM = pl.BlockSpec(memory_space=pltpu.VMEM)
AXES = ("z", "core", "y", "x")
NZ, NC, NY, NX = 8, 2, 8, 4
SHARE = 16
QUAD = 4
BLOCKS = NY * NX // QUAD
TERMS = 2 * 32
UNROLL = 48


def device(z, core, y, x):
    return ((z * NC + core) * NY + y) * NX + x


def turned(i, core, n):
    return i if core == 0 else (n - i) % n


def quad(core, n, f):
    y = (f // 2 * 2 + n // 2 + core) % NY
    x = (f % 2 * 2 + n % 2 + core) % NX
    return y * NX + x


def spot_of(r, core):
    y, x = (r // NX - core) % NY, (r % NX - core) % NX
    return (y % 2 * 2 + x % 2) * BLOCKS + y // 2 * 2 + x // 2


def quad_groups():
    return [
        [device(z, core, *divmod(quad(core, n, f), NX)) for n in range(QUAD)]
        for z in range(NZ)
        for core in range(NC)
        for f in range(BLOCKS)
    ]


def block_groups():
    return [
        [device(z, core, *divmod(quad(core, n, f), NX)) for f in range(BLOCKS)]
        for z in range(NZ)
        for core in range(NC)
        for n in range(QUAD)
    ]


def depth_groups():
    return [
        [device(turned(z, core, NZ), core, y, x) for z in range(NZ)]
        for core in range(NC)
        for y in range(NY)
        for x in range(NX)
    ]


def exchange(x, groups):
    return lax.all_to_all(x, AXES, 0, 0, axis_index_groups=groups, tiled=True)


def place(i, core, n):
    return jnp.where(core == 0, i, (n - i) % n)


def forward_kernel(coords, info, own, other, vals, out, panel, acc):
    tile = vals.shape[1]
    count, core = info[0], info[1]
    for b in range(panel.shape[0] // tile):
        cols = slice(b * tile, (b + 1) * tile)
        for part, owner in ((own, core), (other, 1 - core)):
            slab = jnp.concatenate([part[place(z, owner, NZ), :, cols] for z in range(NZ)], axis=0)
            at = pl.multiple_of(owner * tile, tile)
            panel[cols, pl.ds(at, tile)] = slab.T
    acc[...] = jnp.zeros_like(acc)

    def step(g, carry):
        prods = []
        for u in range(UNROLL):
            s = g * UNROLL + u
            c = pl.multiple_of(coords[2 * s + 1] * tile, tile)
            prods.append(jnp.dot(vals[s], panel[pl.ds(c, tile), :], preferred_element_type=F32))
        for u in range(UNROLL):
            r = coords[2 * (g * UNROLL + u)]
            acc[r] += prods[u]
        return carry

    lax.fori_loop(0, (count + UNROLL - 1) // UNROLL, step, 0)
    for n in range(QUAD):
        for f in range(BLOCKS):
            out[n, f] = acc[n * BLOCKS + f].astype(BF)


def add_kernel(parts, out):
    out[...] = jnp.sum(parts[...].astype(F32), axis=0).astype(BF)


def dense_kernel(info, parts, weight, cot, act, grads, sent, scratch):
    core = info[1]
    width = weight.shape[0]
    order = [(2 * z + c) * SHARE for c in range(NC) for z in range(NZ)]
    s = jnp.sum(parts[...].astype(F32), axis=0).astype(BF)
    w = jnp.concatenate([weight[a : a + SHARE, :] for a in order], axis=0)
    v = jnp.dot(s, w, preferred_element_type=F32)
    k = 0.7978845608028654
    t = jnp.tanh(k * (v + 0.044715 * (v * v * v)))
    act[...] = (0.5 * v * (1.0 + t)).astype(BF)
    slope = 0.5 * (1.0 + t) + 0.5 * v * (1.0 - t * t) * (k * (1.0 + 3.0 * 0.044715 * v * v))
    g = (cot[...].astype(F32) * slope).astype(BF)
    back = lax.dot_general(w, g, (((1,), (1,)), ((), ())), preferred_element_type=F32).astype(BF)
    terms = lax.dot_general(s, g, (((0,), (0,)), ((), ())), preferred_element_type=F32)
    for i, a in enumerate(order):
        scratch[a : a + SHARE, :] = terms[i * SHARE : (i + 1) * SHARE, :]
    half = back.shape[1]
    rows = width // NZ
    grads[...] = back
    for z in range(NZ):
        at = place(z, core, NZ)
        sent[at, :rows, :] = scratch[rows * z : rows * (z + 1), :half].astype(BF)
        sent[at, rows:, :] = scratch[rows * z : rows * (z + 1), half:].astype(BF)


def pack_kernel(grads, terms, sent):
    width = grads.shape[0]
    piece = jnp.sum(terms[...].astype(F32), axis=0).astype(BF)
    for f in range(BLOCKS):
        sent[f, :width, :] = grads[...]
        sent[f, width:, :] = piece


def spread_kernel(got, sent):
    width = got.shape[1] - TERMS
    piece = jnp.sum(got[:, width:, :].astype(F32), axis=0).astype(BF)
    for n in range(QUAD):
        for f in range(BLOCKS):
            sent[n, f * width : (f + 1) * width, :] = got[f, :width, :]
        sent[n, BLOCKS * width :, :] = piece


def backward_kernel(coords, info, panel, vals, mine, theirs, acc):
    count, core = info[0], info[1]
    tiles, width, tile = acc.shape
    acc[...] = jnp.zeros_like(acc)

    def step(g, carry):
        prods = []
        for u in range(UNROLL):
            s = g * UNROLL + u
            spot = coords[2 * s]
            at = pl.multiple_of(lax.rem(spot, BLOCKS) * width, width)
            prods.append(jnp.dot(panel[lax.div(spot, BLOCKS), pl.ds(at, width), :], vals[s], preferred_element_type=F32))
        for u in range(UNROLL):
            c = coords[2 * (g * UNROLL + u) + 1]
            acc[c] += prods[u]
        return carry

    lax.fori_loop(0, (count + UNROLL - 1) // UNROLL, step, 0)
    terms = jnp.sum(panel[:, BLOCKS * width :, :].astype(F32), axis=0).astype(BF)
    for out, owner in ((mine, core), (theirs, 1 - core)):
        for z in range(NZ):
            a = pl.multiple_of(owner * tile + z * SHARE, SHARE)
            at = place(z, owner, NZ)
            for c in range(tiles):
                out[at, SHARE * c : SHARE * (c + 1), :] = acc[c, pl.ds(a, SHARE), :].astype(BF)
            out[at, SHARE * tiles :, :] = terms


def finish_kernel(info, got, grads, weights):
    core = info[1]
    share, tile = SHARE, got.shape[2]
    width = got.shape[1] - TERMS
    rows = TERMS // 2
    total = jnp.sum(got[:, :width, :].astype(F32), axis=0).astype(BF)
    for c in range(width // share):
        grads[:, c * tile : (c + 1) * tile] = total[c * share : (c + 1) * share, :]
    for z in range(NZ):
        at = place(z, core, NZ)
        weights[rows * z : rows * (z + 1), :tile] = got[at, width : width + rows, :].astype(F32)
        weights[rows * z : rows * (z + 1), tile:] = got[at, width + rows :, :].astype(F32)


def params(mib):
    return pltpu.CompilerParams(vmem_limit_bytes=mib * 1024 * 1024)


def body(features, weight, cotangent, tile_values, tile_coords, tile_count):
    core = lax.axis_index("core").astype(jnp.int32)
    nodes, share = features.shape
    slots, tile = tile_values.shape[2:4]
    width = weight.shape[0]
    row_tiles = NY * NX
    col_tiles = nodes // tile
    swap = ((0, 1), (1, 0))

    own = jnp.broadcast_to(features.T[None], (NZ, share, nodes))
    own = exchange(own, depth_groups())
    count, coords = tile_count[0, 0], tile_coords
    coords = jnp.stack([spot_of(coords[0, 0, :, 0], core), coords[0, 0, :, 1]], axis=-1).reshape(-1)
    other = lax.ppermute(own, "core", swap)
    live = lax.broadcasted_iota(jnp.int32, (slots, tile, tile), 0) < count
    vals = jnp.where(live, tile_values[0, 0], jnp.zeros((), BF))
    info = jnp.stack([count, core])
    sums = pl.pallas_call(
        forward_kernel,
        out_shape=jax.ShapeDtypeStruct((QUAD, BLOCKS, tile, width), BF),
        in_specs=[SMEM, SMEM, VMEM, VMEM, VMEM],
        out_specs=VMEM,
        scratch_shapes=[pltpu.VMEM((nodes, width), BF), pltpu.VMEM((row_tiles, tile, width), F32)],
        compiler_params=params(24),
        name="forward_tiles",
    )(coords, info, own, other, vals)
    parts = exchange(sums, quad_groups())
    parts = pl.pallas_call(
        add_kernel,
        out_shape=jax.ShapeDtypeStruct((BLOCKS, tile, width), BF),
        in_specs=[VMEM],
        out_specs=VMEM,
        compiler_params=params(24),
        name="add_quad",
    )(parts)
    parts = exchange(parts, block_groups())
    activations, grads, terms = pl.pallas_call(
        dense_kernel,
        out_shape=(
            jax.ShapeDtypeStruct((tile, width), BF),
            jax.ShapeDtypeStruct((width, tile), BF),
            jax.ShapeDtypeStruct((NZ, TERMS, tile), BF),
        ),
        in_specs=[SMEM, VMEM, VMEM, VMEM],
        out_specs=(VMEM, VMEM, VMEM),
        scratch_shapes=[pltpu.VMEM((width, width), F32)],
        compiler_params=params(24),
        name="dense",
    )(info, parts, weight, cotangent)
    terms = exchange(terms, depth_groups())
    sent = pl.pallas_call(
        pack_kernel,
        out_shape=jax.ShapeDtypeStruct((BLOCKS, width + TERMS, tile), BF),
        in_specs=[VMEM, VMEM],
        out_specs=VMEM,
        compiler_params=params(24),
        name="pack",
    )(grads, terms)
    got = exchange(sent, block_groups())
    sent = pl.pallas_call(
        spread_kernel,
        out_shape=jax.ShapeDtypeStruct((QUAD, BLOCKS * width + TERMS, tile), BF),
        in_specs=[VMEM],
        out_specs=VMEM,
        compiler_params=params(24),
        name="spread_quad",
    )(got)
    panel = exchange(sent, quad_groups())
    mine, theirs = pl.pallas_call(
        backward_kernel,
        out_shape=(jax.ShapeDtypeStruct((NZ, width + TERMS, tile), BF),) * 2,
        in_specs=[SMEM, SMEM, VMEM, VMEM],
        out_specs=(VMEM, VMEM),
        scratch_shapes=[pltpu.VMEM((col_tiles, width, tile), F32)],
        compiler_params=params(24),
        name="backward_tiles",
    )(coords, info, panel, vals)
    got = lax.ppermute(theirs, "core", swap)
    both = (mine.astype(F32) + got.astype(F32)).astype(BF)
    back = exchange(both, depth_groups())
    grad_features, grad_weight = pl.pallas_call(
        finish_kernel,
        out_shape=(jax.ShapeDtypeStruct((share, nodes), BF), jax.ShapeDtypeStruct((width, width), F32)),
        in_specs=[SMEM, VMEM],
        out_specs=(VMEM, VMEM),
        compiler_params=params(24),
        name="finish",
    )(info, back)
    grad_features = grad_features.T
    return (activations, grad_features, grad_weight)


def solution(mesh):
    fine = Mesh(mesh.devices.reshape(NZ, NC, NY, NX), AXES)
    row, col = AXES[:2], AXES[2:]
    placed = (
        P(col, row),
        P(),
        P(row + col, None),
        P(row, col, None, None, None),
        P(row, col, None, None),
        P(row, col),
    )
    return jax.shard_map(
        body,
        mesh=fine,
        in_specs=placed,
        out_specs=(P(row + col, None), P(col, row), P()),
        check_vma=False,
    )
```
